32 devices in a mesh: groups: 2 (over y), dp: 4 (over z), mp: 4 (over x, core).
Axes of the slice: x: 2, y: 2, z: 4, core: 2. Of those that a mesh axis runs over, the one named last changes fastest.
Arguments:
- activations: bfloat16 [1024, 5120], P(('groups', 'dp')), parts along dimension 0, may hold values from -6 to 6
- gradients: bfloat16 [1024, 12800], P(('groups', 'dp')), parts along dimension 0, may hold values from -6 to 6
- input_basis: bfloat16 [5120, 2560], P(None, 'mp'), may hold values from -0.078125 to 0.078125
- output_basis: bfloat16 [12800, 12800], P('dp', 'mp'), may hold values from -0.0546875 to 0.0546875
- lengths: int32 [32], P('groups'), parts along dimension 0, may hold values from 1 to 32, as said below
Outputs:
- corrected_eigenvalues: float32 [5120, 12800], P(('groups', 'dp'), 'mp'), parts along dimension 0
The draws below stay inside these ranges and needn't reach their ends.
There are 2 independent parts, one for each index of `groups`. The reference program is written for one: setup_inputs(seed, part) draws one part's arguments, and reference() takes and returns one part's arrays. A program takes and returns all parts, laid end to end along the dimension named above; an argument that names none is the same for every part. Nothing has to cross between parts.
Inputs may be any that keep to these rules, and one draw needn't show every extreme that they name: `lengths`: at least one sequence has exactly 32 tokens.
All inputs are finite; a program needn't handle non-finite values.
Results may differ from the reference program's by a relative error of at most 0.012.
Values may be sent and summed in bfloat16 or wider, within the bound.
No kernel may reach another device: no remote copies, remote signals or barrier semaphores. Data moves between devices by JAX's collectives and lax.ppermute only.
A program may use at most 320 MiB of HBM per device.

```python
import jax
import jax.numpy as jnp
from jax import lax

D = 5120
HID = 12800
KA = 2560
KG = 12800
TOK_DEV = 128
SEQ_DEV = 4
TOKENS = 512
SEQS = 16
N_DP = 4


def draw_lengths(key, part):
    key = jax.random.fold_in(key, 7)
    longest = TOK_DEV // SEQ_DEV
    values = jax.random.randint(key, (SEQS,), 1, longest + 1, dtype=jnp.int32)
    position = jax.random.randint(jax.random.fold_in(key, 1), (), 0, SEQS, dtype=jnp.int32)
    return jnp.where(jnp.arange(SEQS, dtype=jnp.int32) == position, jnp.int32(longest), values)


def shard_levels(stream_key, dims, cuts, smallest, top_value):
    def one(axis_at, shards_of):
        steps = jax.random.uniform(jax.random.fold_in(jax.random.fold_in(stream_key, 6), axis_at), (shards_of,), jnp.float32, smallest / len(cuts), top_value / len(cuts))
        return jnp.repeat(jnp.exp(steps), dims[axis_at] // shards_of).reshape((-1,) + (1,) * (len(dims) - axis_at - 1))

    factor_of = one(*cuts[0])
    for cut in cuts[1:]:
        factor_of = factor_of * one(*cut)
    return factor_of


def noise(rng, dims, spread, limit, pieces=(), held_as=jnp.bfloat16):
    entries = spread * jax.random.normal(rng, dims, jnp.float32)
    if pieces:
        entries = entries * shard_levels(rng, dims, pieces, -0.22, 0.18)
    return jnp.clip(entries, -limit, limit).astype(held_as)


def setup_inputs(seed: int = 0, part: int = 0) -> dict:
    streams_of = jax.random.split(jax.random.key(seed), 6)
    part_keys = jax.random.split(jax.random.fold_in(streams_of[5], part), 6)
    return {
        "activations": noise(part_keys[0], (TOKENS, D), 1.0, 6.0, ((0, 4),)),
        "gradients": noise(part_keys[1], (TOKENS, HID), 1.0, 6.0, ((0, 4),)),
        "input_basis": noise(streams_of[2], (D, KA), D ** -0.5, 0.078125, ((1, 4),)),
        "output_basis": noise(streams_of[3], (HID, KG), HID ** -0.5, 0.0546875, ((0, 4), (1, 4))),
        "lengths": draw_lengths(jax.random.fold_in(jax.random.fold_in(streams_of[5], part), 71), part),
    }


def seq_squares(at_rows, gt_rows, seq_lengths):
    row_total = at_rows.shape[0]
    seq_ends = jnp.cumsum(seq_lengths, dtype=jnp.int32)
    starts = seq_ends - seq_lengths
    row_ids = jnp.arange(row_total, dtype=jnp.int32)[:, None]
    inside = (row_ids >= starts[None, :]) & (row_ids < seq_ends[None, :])
    totals = jnp.zeros((at_rows.shape[1], gt_rows.shape[1]), jnp.float32)
    for member in range(seq_lengths.shape[0]):
        masked = jnp.where(inside[:, member:member + 1], at_rows, jnp.zeros_like(at_rows))
        summed = lax.dot_general(masked, gt_rows, (((0,), (0,)), ((), ())), preferred_element_type=jnp.float32)
        totals = totals + summed * summed
    return totals


def reference(activations, gradients, input_basis, output_basis, lengths):
    rotated_in = jnp.dot(activations, input_basis, preferred_element_type=jnp.float32).astype(jnp.bfloat16)
    block_width = HID // N_DP
    accum = jnp.zeros((TOKENS, KG), jnp.float32)
    for block in range(N_DP):
        part = jnp.dot(gradients[:, block * block_width:(block + 1) * block_width],
                       output_basis[block * block_width:(block + 1) * block_width, :],
                       preferred_element_type=jnp.float32).astype(jnp.bfloat16)
        part = lax.optimization_barrier(part)
        accum = accum + part.astype(jnp.float32)
    rotated_out = accum.astype(jnp.bfloat16)

    def add_shard(shard, running):
        row_start = (shard * TOK_DEV).astype(jnp.int32)
        at_rows = lax.dynamic_slice_in_dim(rotated_in, row_start, TOK_DEV, 0)
        gt_rows = lax.dynamic_slice_in_dim(rotated_out, row_start, TOK_DEV, 0)
        seq_lengths = lax.dynamic_slice_in_dim(lengths, (shard * SEQ_DEV).astype(jnp.int32), SEQ_DEV, 0)
        return running + seq_squares(at_rows, gt_rows, seq_lengths)

    result = lax.fori_loop(jnp.int32(0), jnp.int32(N_DP), add_shard, jnp.zeros((KA, KG), jnp.float32))
    return result * (1.0 / (TOK_DEV * N_DP))
```

```python
import functools

import jax
import jax.numpy as jnp
from jax import lax
from jax.experimental import pallas as pl
from jax.experimental.pallas import tpu as pltpu
from jax.sharding import PartitionSpec as P

TILE = 256
WINDOW = 128
ALIGN = 16
VMEM_LIMIT = 48 * 1024 * 1024


def column_chunks(width):
    tiles = -(-width // TILE)
    count = min(5, tiles)
    edges = [tiles * c // count for c in range(count + 1)]
    return [
        (lo * TILE, min(hi * TILE, width) - lo * TILE) for lo, hi in zip(edges[:-1], edges[1:])
    ]


def compact_kernel(tgt, lim, pieces, *refs):
    sources, out, buf, sems = refs[: len(pieces)], refs[-3], refs[-2], refs[-1]
    copies = []
    row = 0
    for j, size in enumerate(pieces):
        copies.append(pltpu.make_async_copy(sources[j], buf.at[pl.ds(row, size)], sems.at[j]))
        copies[-1].start()
        row += size
    selectors = []
    for j, size in enumerate(pieces):
        place = lax.broadcasted_iota(jnp.int32, (out.shape[0], size), 0)
        token = lax.broadcasted_iota(jnp.int32, (out.shape[0], size), 1) + tgt[j]
        selectors.append(jnp.where((place == token) & (place < lim[j]), 1.0, 0.0))
    selector = jnp.concatenate(selectors, axis=1).astype(jnp.bfloat16)
    for copy in copies:
        copy.wait()
    width = out.shape[1]
    step = 640 if width % 640 == 0 else width
    for lo in range(0, width, step):
        out[:, lo : lo + step] = jnp.dot(
            selector, buf[:, lo : lo + step], preferred_element_type=jnp.float32
        ).astype(out.dtype)


def compact(pieces, targets, limits, rows):
    sizes = tuple(p.shape[0] for p in pieces)
    width = pieces[0].shape[1]

    def kernel(tgt, lim, *refs):
        compact_kernel(tgt, lim, sizes, *refs)

    return pl.pallas_call(
        kernel,
        grid_spec=pltpu.PrefetchScalarGridSpec(
            num_scalar_prefetch=2,
            grid=(),
            in_specs=[pl.BlockSpec(memory_space=pl.ANY)] * len(pieces),
            out_specs=pl.BlockSpec(memory_space=pltpu.VMEM),
            scratch_shapes=[
                pltpu.VMEM((sum(sizes), width), jnp.bfloat16),
                pltpu.SemaphoreType.DMA((len(pieces),)),
            ],
        ),
        out_shape=jax.ShapeDtypeStruct((rows, width), jnp.bfloat16),
        compiler_params=pltpu.CompilerParams(vmem_limit_bytes=VMEM_LIMIT),
        name="compact_rows",
    )(targets, limits, *pieces)


def rotate_kernel(rows_ref, basis_ref, out_ref):
    out_ref[...] = jnp.dot(
        rows_ref[...], basis_ref[...], preferred_element_type=jnp.float32
    ).astype(out_ref.dtype)


def rotate(rows, basis, first, size):
    depth = basis.shape[0]
    begin = first // TILE
    return pl.pallas_call(
        rotate_kernel,
        grid=(-(-size // TILE),),
        in_specs=[
            pl.BlockSpec(rows.shape, lambda j: (0, 0)),
            pl.BlockSpec((depth, TILE), lambda j: (0, begin + j)),
        ],
        out_specs=pl.BlockSpec((rows.shape[0], TILE), lambda j: (0, j)),
        out_shape=jax.ShapeDtypeStruct((rows.shape[0], size), jnp.bfloat16),
        compiler_params=pltpu.CompilerParams(vmem_limit_bytes=VMEM_LIMIT),
        cost_estimate=pl.CostEstimate(
            flops=2 * rows.shape[0] * depth * size,
            bytes_accessed=2 * depth * size + 2 * rows.size,
            transcendentals=0,
        ),
        name="rotate_chunk",
    )(rows, basis)


def squares_kernel(seqs, scale, window_starts, at_ref, gt_ref, *refs):
    out_ref = refs[-1]
    for n in range(seqs):
        start = pl.multiple_of(window_starts[n], ALIGN)
        summed = jnp.dot(
            at_ref[:, n * WINDOW : (n + 1) * WINDOW],
            gt_ref[pl.ds(start, WINDOW), :],
            preferred_element_type=jnp.float32,
        )
        squared = summed * summed
        if n == 0:
            out_ref[...] = squared
        elif n < seqs - 1:
            out_ref[...] += squared
        else:
            out_ref[...] = (out_ref[...] + squared) * scale


def squares(window_starts, at_windows, gt_chunk, scale, first, total_width, previous):
    seqs = window_starts.shape[0]
    directions = at_windows.shape[0]
    rows, size = gt_chunk.shape
    begin = first // TILE
    in_specs = [
        pl.BlockSpec(at_windows.shape, lambda j, ws: (0, 0)),
        pl.BlockSpec((rows, TILE), lambda j, ws: (0, j)),
    ]
    operands = [window_starts, at_windows, gt_chunk]
    aliases = {}
    if previous is not None:
        in_specs.append(pl.BlockSpec(memory_space=pl.ANY))
        operands.append(previous)
        aliases = {3: 0}
    return pl.pallas_call(
        functools.partial(squares_kernel, seqs, scale),
        grid_spec=pltpu.PrefetchScalarGridSpec(
            num_scalar_prefetch=1,
            grid=(-(-size // TILE),),
            in_specs=in_specs,
            out_specs=pl.BlockSpec((directions, TILE), lambda j, ws: (0, begin + j)),
        ),
        out_shape=jax.ShapeDtypeStruct((directions, total_width), jnp.float32),
        input_output_aliases=aliases,
        compiler_params=pltpu.CompilerParams(vmem_limit_bytes=VMEM_LIMIT),
        cost_estimate=pl.CostEstimate(
            flops=2 * seqs * directions * size * WINDOW,
            bytes_accessed=4 * directions * size + 2 * rows * size,
            transcendentals=0,
        ),
        name="sum_squares",
    )(*operands)


def add_rounded(a, b):
    return (a.astype(jnp.float32) + b.astype(jnp.float32)).astype(jnp.bfloat16)


def exchange_gradients(gradients, shards, parts):
    d, m = lax.axis_index("dp"), lax.axis_index("mp")
    rows, hidden = gradients.shape
    width = hidden // shards
    if shards == 4 and parts == 4:
        share = rows // parts
        mine = lax.dynamic_slice_in_dim(gradients, m * share, share, 0)
        own = lax.dynamic_slice_in_dim(gradients, d * width, width, 1)
        pieces = [(own, d, 0)]
        far = []
        for k in (2, 1, 3):
            block = lax.dynamic_slice_in_dim(mine, lax.rem(d + k, shards) * width, width, 1)
            received = lax.ppermute(block, "dp", [(e, (e + k) % shards) for e in range(shards)])
            far.append((received, lax.rem(d + shards - k, shards)))
        for received, e in far:
            crossed = lax.ppermute(received, "mp", [(p, p ^ 2) for p in range(parts)])
            pieces.append((received, e, m * share))
            pieces.append((crossed, e, (m ^ 2) * share))
            for piece, part in ((received, m ^ 1), (crossed, m ^ 3)):
                swapped = lax.ppermute(piece, "mp", [(p, p ^ 1) for p in range(parts)])
                pieces.append((swapped, e, part * share))
        return pieces
    exchanged = lax.all_to_all(gradients, "dp", split_axis=1, concat_axis=0, tiled=True)
    return [(exchanged[e * rows : (e + 1) * rows], e, 0) for e in range(shards)]


def exchange_inputs(rotated_in, shards, parts):
    d, m = lax.axis_index("dp"), lax.axis_index("mp")
    if shards == 4 and parts == 4:
        at = lambda e, p: e * parts + p
        gathered = [rotated_in]
        for k in range(1, shards):
            pairs = [(at((p + k) % shards, p), at(p, p)) for p in range(parts)]
            gathered.append(lax.ppermute(rotated_in, ("dp", "mp"), pairs))
        held = jnp.concatenate(gathered, axis=0)
        crossed = lax.ppermute(held, ("dp", "mp"), [(at(p, p), at(p, p ^ 2)) for p in range(parts)])
        held = jnp.where(m == d, held, crossed)
        swapped = lax.ppermute(
            held,
            ("dp", "mp"),
            [(at(p, p), at(p, p ^ 1)) for p in range(parts)]
            + [(at(p, p ^ 2), at(p, p ^ 3)) for p in range(parts)],
        )
        held = jnp.where((m == d) | (m == (d ^ 2)), held, swapped)
        return held, lax.rem(d + jnp.arange(shards, dtype=jnp.int32), shards)
    full = lax.all_gather(rotated_in, "mp", axis=1, tiled=True)
    held = lax.all_to_all(full, "dp", split_axis=1, concat_axis=0, tiled=True)
    return held, jnp.arange(shards, dtype=jnp.int32)


def sum_over_shards(parts, shards):
    if shards != 4:
        return [lax.psum(part, "dp") for part in parts]
    d = lax.axis_index("dp")
    middle = (d == 1) | (d == 2)
    sums = []
    for part in parts:
        pair = add_rounded(part, lax.ppermute(part, "dp", [(0, 1), (3, 2)]))
        both = add_rounded(pair, lax.ppermute(pair, "dp", [(1, 2), (2, 1)]))
        sums.append(jnp.where(middle, both, lax.ppermute(both, "dp", [(1, 0), (2, 3)])))
    return sums


def per_device(activations, gradients, input_basis, output_basis, lengths):
    shards, parts = lax.axis_size("dp"), lax.axis_size("mp")
    shard_rows = activations.shape[0]
    rows = shard_rows * shards
    seqs = lengths.shape[0]
    per_shard = seqs // shards

    seq_ends = jnp.cumsum(lengths, dtype=jnp.int32)
    seq_starts = seq_ends - lengths
    shard_ends = seq_ends[per_shard - 1 :: per_shard]
    shard_starts = seq_starts[::per_shard]
    window_starts = jnp.minimum(seq_starts // ALIGN * ALIGN, rows - WINDOW)

    pieces = exchange_gradients(gradients, shards, parts)
    rotated_in = jnp.dot(activations, input_basis, preferred_element_type=jnp.float32).astype(
        jnp.bfloat16
    )
    held, order = exchange_inputs(rotated_in, shards, parts)

    piece_shards = jnp.stack([jnp.asarray(e, jnp.int32) for _, e, _ in pieces])
    piece_rows = jnp.stack([jnp.asarray(r, jnp.int32) for _, _, r in pieces])
    targets = shard_starts[piece_shards] + piece_rows
    limits = shard_ends[piece_shards]
    compacted = compact([p for p, _, _ in pieces], targets, limits, rows)

    place = window_starts[:, None] + jnp.arange(WINDOW, dtype=jnp.int32)[None, :]
    inside = (place >= seq_starts[:, None]) & (place < seq_ends[:, None])
    seq_shard = jnp.arange(seqs, dtype=jnp.int32)[:, None] // per_shard
    token = place - jnp.repeat(shard_starts, per_shard)[:, None] + seq_shard * shard_rows
    token = jnp.where(inside, token, -1).reshape(-1)
    held_token = (
        order[:, None] * shard_rows + jnp.arange(shard_rows, dtype=jnp.int32)[None, :]
    ).reshape(-1)
    selector = (held_token[:, None] == token[None, :]).astype(jnp.bfloat16)
    at_windows = lax.dot_general(
        held, selector, (((0,), (0,)), ((), ())), preferred_element_type=jnp.float32
    ).astype(jnp.bfloat16)

    width = output_basis.shape[1]
    chunks = column_chunks(width)
    partials = [rotate(compacted, output_basis, first, size) for first, size in chunks]
    result = None
    for (first, _), gt_chunk in zip(chunks, sum_over_shards(partials, shards)):
        result = squares(window_starts, at_windows, gt_chunk, 1.0 / rows, first, width, result)
    return result


def solution(mesh):
    placed = (
        P(("groups", "dp"), None),
        P(("groups", "dp"), None),
        P(None, "mp"),
        P("dp", "mp"),
        P("groups"),
    )
    return jax.shard_map(
        per_device, mesh=mesh, in_specs=placed, out_specs=P(("groups", "dp"), "mp"), check_vma=False
    )
```

```python
import functools

import jax
import jax.numpy as jnp
from jax import lax
from jax.experimental import pallas as pl
from jax.experimental.pallas import tpu as pltpu
from jax.sharding import PartitionSpec as P

TILE = 256
WINDOW = 128
ALIGN = 16
VMEM_LIMIT = 48 * 1024 * 1024


def column_chunks(width):
    tiles = -(-width // TILE)
    count = min(5, tiles)
    edges = [tiles * c // count for c in range(count + 1)]
    return [
        (lo * TILE, min(hi * TILE, width) - lo * TILE) for lo, hi in zip(edges[:-1], edges[1:])
    ]


def compact_kernel(pieces, place_ref, *refs):
    sources, out, buf, sems = refs[: len(pieces)], refs[-3], refs[-2], refs[-1]
    copies = []
    row = 0
    for j, size in enumerate(pieces):
        copies.append(pltpu.make_async_copy(sources[j], buf.at[pl.ds(row, size)], sems.at[j]))
        copies[-1].start()
        row += size
    place = lax.broadcasted_iota(jnp.int32, (out.shape[0], row), 0)
    selector = jnp.where(place == place_ref[...], 1.0, 0.0).astype(jnp.bfloat16)
    for copy in copies:
        copy.wait()
    width = out.shape[1]
    step = 640 if width % 640 == 0 else width
    for lo in range(0, width, step):
        out[:, lo : lo + step] = jnp.dot(
            selector, buf[:, lo : lo + step], preferred_element_type=jnp.float32
        ).astype(out.dtype)


def compact(pieces, places, rows):
    sizes = tuple(p.shape[0] for p in pieces)
    width = pieces[0].shape[1]
    return pl.pallas_call(
        functools.partial(compact_kernel, sizes),
        in_specs=[pl.BlockSpec(memory_space=pltpu.VMEM)]
        + [pl.BlockSpec(memory_space=pl.ANY)] * len(pieces),
        out_specs=pl.BlockSpec(memory_space=pltpu.VMEM),
        scratch_shapes=[
            pltpu.VMEM((sum(sizes), width), jnp.bfloat16),
            pltpu.SemaphoreType.DMA((len(pieces),)),
        ],
        out_shape=jax.ShapeDtypeStruct((rows, width), jnp.bfloat16),
        compiler_params=pltpu.CompilerParams(vmem_limit_bytes=VMEM_LIMIT),
        name="compact_rows",
    )(places[None, :], *pieces)


def rotate_kernel(rows_ref, basis_ref, out_ref):
    out_ref[...] = jnp.dot(
        rows_ref[...], basis_ref[...], preferred_element_type=jnp.float32
    ).astype(out_ref.dtype)


def rotate(rows, basis, first, size):
    depth = basis.shape[0]
    begin = first // TILE
    return pl.pallas_call(
        rotate_kernel,
        grid=(-(-size // TILE),),
        in_specs=[
            pl.BlockSpec(rows.shape, lambda j: (0, 0)),
            pl.BlockSpec((depth, TILE), lambda j: (0, begin + j)),
        ],
        out_specs=pl.BlockSpec((rows.shape[0], TILE), lambda j: (0, j)),
        out_shape=jax.ShapeDtypeStruct((rows.shape[0], size), jnp.bfloat16),
        compiler_params=pltpu.CompilerParams(vmem_limit_bytes=VMEM_LIMIT),
        cost_estimate=pl.CostEstimate(
            flops=2 * rows.shape[0] * depth * size,
            bytes_accessed=2 * depth * size + 2 * rows.size,
            transcendentals=0,
        ),
        name="rotate_chunk",
    )(rows, basis)


def squares_kernel(seqs, scale, window_starts, at_ref, gt_ref, *refs):
    out_ref = refs[-1]
    for n in range(seqs):
        start = pl.multiple_of(window_starts[n], ALIGN)
        summed = jnp.dot(
            at_ref[:, n * WINDOW : (n + 1) * WINDOW],
            gt_ref[pl.ds(start, WINDOW), :],
            preferred_element_type=jnp.float32,
        )
        squared = summed * summed
        if n == 0:
            out_ref[...] = squared
        elif n < seqs - 1:
            out_ref[...] += squared
        else:
            out_ref[...] = (out_ref[...] + squared) * scale


def squares(window_starts, at_windows, gt_chunk, scale, first, total_width, previous):
    seqs = window_starts.shape[0]
    directions = at_windows.shape[0]
    rows, size = gt_chunk.shape
    begin = first // TILE
    in_specs = [
        pl.BlockSpec(at_windows.shape, lambda j, ws: (0, 0)),
        pl.BlockSpec((rows, TILE), lambda j, ws: (0, j)),
    ]
    operands = [window_starts, at_windows, gt_chunk]
    aliases = {}
    if previous is not None:
        in_specs.append(pl.BlockSpec(memory_space=pl.ANY))
        operands.append(previous)
        aliases = {3: 0}
    return pl.pallas_call(
        functools.partial(squares_kernel, seqs, scale),
        grid_spec=pltpu.PrefetchScalarGridSpec(
            num_scalar_prefetch=1,
            grid=(-(-size // TILE),),
            in_specs=in_specs,
            out_specs=pl.BlockSpec((directions, TILE), lambda j, ws: (0, begin + j)),
        ),
        out_shape=jax.ShapeDtypeStruct((directions, total_width), jnp.float32),
        input_output_aliases=aliases,
        compiler_params=pltpu.CompilerParams(vmem_limit_bytes=VMEM_LIMIT),
        cost_estimate=pl.CostEstimate(
            flops=2 * seqs * directions * size * WINDOW,
            bytes_accessed=4 * directions * size + 2 * rows * size,
            transcendentals=0,
        ),
        name="sum_squares",
    )(*operands)


def add_rounded(a, b):
    return (a.astype(jnp.float32) + b.astype(jnp.float32)).astype(jnp.bfloat16)


def exchange_gradients(gradients, shards, parts):
    d, m = lax.axis_index("dp"), lax.axis_index("mp")
    rows, hidden = gradients.shape
    width = hidden // shards
    if shards == 4 and parts == 4:
        share = rows // parts
        mine = lax.dynamic_slice_in_dim(gradients, m * share, share, 0)
        own = lax.dynamic_slice_in_dim(gradients, d * width, width, 1)
        pieces = [(own, d, 0)]
        far, sent = [], []
        for k in (2, 1, 3):
            block = lax.dynamic_slice_in_dim(mine, lax.rem(d + k, shards) * width, width, 1)
            sent.append(block)
            received = lax.ppermute(block, "dp", [(e, (e + k) % shards) for e in range(shards)])
            far.append((received, lax.rem(d + shards - k, shards)))
        for received, e in far:
            crossed = lax.ppermute(received, "mp", [(p, p ^ 2) for p in range(parts)])
            pieces.append((received, e, m * share))
            pieces.append((crossed, e, (m ^ 2) * share))
            for piece, part in ((received, m ^ 1), (crossed, m ^ 3)):
                swapped = lax.ppermute(piece, "mp", [(p, p ^ 1) for p in range(parts)])
                pieces.append((swapped, e, part * share))
        return pieces, sent
    exchanged = lax.all_to_all(gradients, "dp", split_axis=1, concat_axis=0, tiled=True)
    return [(exchanged[e * rows : (e + 1) * rows], e, 0) for e in range(shards)], []


def exchange_inputs(rotated_in, shards, parts):
    d, m = lax.axis_index("dp"), lax.axis_index("mp")
    if shards == 4 and parts == 4:
        at = lambda e, p: e * parts + p
        gathered = [rotated_in]
        for k in range(1, shards):
            pairs = [(at((p + k) % shards, p), at(p, p)) for p in range(parts)]
            gathered.append(lax.ppermute(rotated_in, ("dp", "mp"), pairs))
        held = jnp.concatenate(gathered, axis=0)
        crossed = lax.ppermute(held, ("dp", "mp"), [(at(p, p), at(p, p ^ 2)) for p in range(parts)])
        held = jnp.where(m == d, held, crossed)
        swapped = lax.ppermute(
            held,
            ("dp", "mp"),
            [(at(p, p), at(p, p ^ 1)) for p in range(parts)]
            + [(at(p, p ^ 2), at(p, p ^ 3)) for p in range(parts)],
        )
        held = jnp.where((m == d) | (m == (d ^ 2)), held, swapped)
        return held, lax.rem(d + jnp.arange(shards, dtype=jnp.int32), shards)
    full = lax.all_gather(rotated_in, "mp", axis=1, tiled=True)
    held = lax.all_to_all(full, "dp", split_axis=1, concat_axis=0, tiled=True)
    return held, jnp.arange(shards, dtype=jnp.int32)


def after(x, *others):
    others = [o for o in others if o is not None]
    return lax.optimization_barrier((x, *others))[0] if others else x


def sum_over_shards(parts, shards):
    if shards != 4:
        return [lax.psum(part, "dp") for part in parts]
    d = lax.axis_index("dp")
    middle = (d == 1) | (d == 2)
    count = len(parts)
    inward = [lax.ppermute(part, "dp", [(0, 1), (3, 2)]) for part in parts]
    pairs, across, sums, outward, done = {}, {}, {}, {}, {}
    for s in range(count + 2):
        if s < count:
            pairs[s] = add_rounded(parts[s], after(inward[s], sums.get(s - 2)))
            across[s] = lax.ppermute(pairs[s], "dp", [(1, 2), (2, 1)])
        if 1 <= s <= count:
            sums[s - 1] = add_rounded(pairs[s - 1], after(across[s - 1], pairs.get(s)))
            outward[s - 1] = lax.ppermute(sums[s - 1], "dp", [(1, 0), (2, 3)])
        if s >= 2:
            got = after(outward[s - 2], sums.get(s - 1))
            done[s - 2] = jnp.where(middle, sums[s - 2], got)
    return [done[c] for c in range(count)]


def per_device(activations, gradients, input_basis, output_basis, lengths):
    shards, parts = lax.axis_size("dp"), lax.axis_size("mp")
    shard_rows = activations.shape[0]
    rows = shard_rows * shards
    seqs = lengths.shape[0]
    per_shard = seqs // shards

    seq_ends = jnp.cumsum(lengths, dtype=jnp.int32)
    seq_starts = seq_ends - lengths
    shard_ends = seq_ends[per_shard - 1 :: per_shard]
    shard_starts = seq_starts[::per_shard]
    window_starts = jnp.minimum(seq_starts // ALIGN * ALIGN, rows - WINDOW)

    pieces, sent = exchange_gradients(gradients, shards, parts)
    activations = after(activations, *sent)
    rotated_in = jnp.dot(activations, input_basis, preferred_element_type=jnp.float32).astype(
        jnp.bfloat16
    )
    held, order = exchange_inputs(rotated_in, shards, parts)

    places = []
    for piece, e, row in pieces:
        start = lax.dynamic_index_in_dim(shard_starts, e, keepdims=False)
        end = lax.dynamic_index_in_dim(shard_ends, e, keepdims=False)
        place = start + row + jnp.arange(piece.shape[0], dtype=jnp.int32)
        places.append(jnp.where(place < end, place, -1))
    compacted = compact([p for p, _, _ in pieces], jnp.concatenate(places), rows)

    place = window_starts[:, None] + jnp.arange(WINDOW, dtype=jnp.int32)[None, :]
    inside = (place >= seq_starts[:, None]) & (place < seq_ends[:, None])
    seq_shard = jnp.arange(seqs, dtype=jnp.int32)[:, None] // per_shard
    token = place - jnp.repeat(shard_starts, per_shard)[:, None] + seq_shard * shard_rows
    token = jnp.where(inside, token, -1).reshape(-1)
    held_token = (
        order[:, None] * shard_rows + jnp.arange(shard_rows, dtype=jnp.int32)[None, :]
    ).reshape(-1)
    selector = (held_token[:, None] == token[None, :]).astype(jnp.bfloat16)
    at_windows = lax.dot_general(
        held, selector, (((0,), (0,)), ((), ())), preferred_element_type=jnp.float32
    ).astype(jnp.bfloat16)

    width = output_basis.shape[1]
    chunks = column_chunks(width)
    partials = []
    for first, size in chunks:
        source = after(compacted, *partials[-1:])
        partials.append(rotate(source, output_basis, first, size))
    result = None
    for (first, _), gt_chunk in zip(chunks, sum_over_shards(partials, shards)):
        result = squares(window_starts, at_windows, gt_chunk, 1.0 / rows, first, width, result)
    return result


def solution(mesh):
    placed = (
        P(("groups", "dp"), None),
        P(("groups", "dp"), None),
        P(None, "mp"),
        P("dp", "mp"),
        P("groups"),
    )
    return jax.shard_map(
        per_device, mesh=mesh, in_specs=placed, out_specs=P(("groups", "dp"), "mp"), check_vma=False
    )
```

```python
import functools

import jax
import jax.numpy as jnp
from jax import lax
from jax.experimental import pallas as pl
from jax.experimental.pallas import tpu as pltpu
from jax.sharding import PartitionSpec as P

TILE = 256
WINDOW = 128
ALIGN = 16
AHEAD = 3
MIB = 1024 * 1024


def column_chunks(width):
    tiles = -(-width // TILE)
    count = min(5, tiles)
    edges = [tiles * c // count for c in range(count + 1)]
    return [
        (lo * TILE, min(hi * TILE, width) - lo * TILE) for lo, hi in zip(edges[:-1], edges[1:])
    ]


def compact_kernel(pieces, place_ref, *refs):
    sources, out, buf, sems = refs[: len(pieces)], refs[-3], refs[-2], refs[-1]
    copies = []
    row = 0
    for j, size in enumerate(pieces):
        copies.append(pltpu.make_async_copy(sources[j], buf.at[pl.ds(row, size)], sems.at[j]))
        copies[-1].start()
        row += size
    place = lax.broadcasted_iota(jnp.int32, (out.shape[0], row), 0)
    selector = jnp.where(place == place_ref[...], 1.0, 0.0).astype(jnp.bfloat16)
    for copy in copies:
        copy.wait()
    width = out.shape[1]
    step = 640 if width % 640 == 0 else width
    for lo in range(0, width, step):
        out[:, lo : lo + step] = jnp.dot(
            selector, buf[:, lo : lo + step], preferred_element_type=jnp.float32
        ).astype(out.dtype)


def compact(pieces, places, rows):
    sizes = tuple(p.shape[0] for p in pieces)
    width = pieces[0].shape[1]
    return pl.pallas_call(
        functools.partial(compact_kernel, sizes),
        in_specs=[pl.BlockSpec(memory_space=pltpu.VMEM)]
        + [pl.BlockSpec(memory_space=pl.ANY)] * len(pieces),
        out_specs=pl.BlockSpec(memory_space=pltpu.VMEM),
        scratch_shapes=[
            pltpu.VMEM((sum(sizes), width), jnp.bfloat16),
            pltpu.SemaphoreType.DMA((len(pieces),)),
        ],
        out_shape=jax.ShapeDtypeStruct((rows, width), jnp.bfloat16),
        compiler_params=pltpu.CompilerParams(
            vmem_limit_bytes=2 * width * (sum(sizes) + rows) + 8 * rows * sum(sizes) + 6 * MIB
        ),
        name="compact_rows",
    )(places[None, :], *pieces)


def rotate_kernel(rows_ref, basis_ref, out_ref):
    out_ref[...] = jnp.dot(
        rows_ref[...], basis_ref[...], preferred_element_type=jnp.float32
    ).astype(out_ref.dtype)


def rotate(rows, basis, first, size):
    depth = basis.shape[0]
    begin = first // TILE
    return pl.pallas_call(
        rotate_kernel,
        grid=(-(-size // TILE),),
        in_specs=[
            pl.BlockSpec(rows.shape, lambda j: (0, 0)),
            pl.BlockSpec((depth, TILE), lambda j: (0, begin + j)),
        ],
        out_specs=pl.BlockSpec((rows.shape[0], TILE), lambda j: (0, j)),
        out_shape=jax.ShapeDtypeStruct((rows.shape[0], size), jnp.bfloat16),
        compiler_params=pltpu.CompilerParams(
            vmem_limit_bytes=4 * (rows.size + depth * TILE) + 4 * rows.shape[0] * TILE + 6 * MIB
        ),
        cost_estimate=pl.CostEstimate(
            flops=2 * rows.shape[0] * depth * size,
            bytes_accessed=2 * depth * size + 2 * rows.size,
            transcendentals=0,
        ),
        name="rotate_chunk",
    )(rows, basis)


def squares_kernel(seqs, scale, window_starts, at_ref, gt_ref, *refs):
    out_ref = refs[-1]
    for n in range(seqs):
        start = pl.multiple_of(window_starts[n], ALIGN)
        summed = jnp.dot(
            at_ref[:, n * WINDOW : (n + 1) * WINDOW],
            gt_ref[pl.ds(start, WINDOW), :],
            preferred_element_type=jnp.float32,
        )
        squared = summed * summed
        if n == 0:
            out_ref[...] = squared
        elif n < seqs - 1:
            out_ref[...] += squared
        else:
            out_ref[...] = (out_ref[...] + squared) * scale


def squares(window_starts, at_windows, gt_chunk, scale, first, total_width, previous):
    seqs = window_starts.shape[0]
    directions = at_windows.shape[0]
    rows, size = gt_chunk.shape
    begin = first // TILE
    in_specs = [
        pl.BlockSpec(at_windows.shape, lambda j, ws: (0, 0)),
        pl.BlockSpec((rows, TILE), lambda j, ws: (0, j)),
    ]
    operands = [window_starts, at_windows, gt_chunk]
    aliases = {}
    if previous is not None:
        in_specs.append(pl.BlockSpec(memory_space=pl.ANY))
        operands.append(previous)
        aliases = {3: 0}
    return pl.pallas_call(
        functools.partial(squares_kernel, seqs, scale),
        grid_spec=pltpu.PrefetchScalarGridSpec(
            num_scalar_prefetch=1,
            grid=(-(-size // TILE),),
            in_specs=in_specs,
            out_specs=pl.BlockSpec((directions, TILE), lambda j, ws: (0, begin + j)),
        ),
        out_shape=jax.ShapeDtypeStruct((directions, total_width), jnp.float32),
        input_output_aliases=aliases,
        compiler_params=pltpu.CompilerParams(
            vmem_limit_bytes=4 * (at_windows.size + rows * TILE) + 16 * directions * TILE + 6 * MIB
        ),
        cost_estimate=pl.CostEstimate(
            flops=2 * seqs * directions * size * WINDOW,
            bytes_accessed=4 * directions * size + 2 * rows * size,
            transcendentals=0,
        ),
        name="sum_squares",
    )(*operands)


def add_rounded(a, b):
    return (a.astype(jnp.float32) + b.astype(jnp.float32)).astype(jnp.bfloat16)


def exchange_gradients(gradients, shards, parts):
    d, m = lax.axis_index("dp"), lax.axis_index("mp")
    rows, hidden = gradients.shape
    width = hidden // shards
    if shards == 4 and parts == 4:
        share = rows // parts
        mine = lax.dynamic_slice_in_dim(gradients, m * share, share, 0)
        own = lax.dynamic_slice_in_dim(gradients, d * width, width, 1)
        pieces, flips, steps = [own], [], []
        far, sent = [], []
        for k in (2, 1, 3):
            block = lax.dynamic_slice_in_dim(mine, lax.rem(d + k, shards) * width, width, 1)
            sent.append(block)
            far.append(lax.ppermute(block, "dp", [(e, (e + k) % shards) for e in range(shards)]))
        for k, received in zip((2, 1, 3), far):
            crossed = lax.ppermute(received, "mp", [(p, p ^ 2) for p in range(parts)])
            pieces += [received, crossed]
            for piece in (received, crossed):
                pieces.append(lax.ppermute(piece, "mp", [(p, p ^ 1) for p in range(parts)]))
            flips += [0, 2, 1, 3]
            steps += [k] * parts
        row = jnp.arange(rows * shards, dtype=jnp.int32)
        group = jnp.maximum(row - rows, 0) // share
        flip = sum(jnp.where(group == g, f, 0) for g, f in enumerate(flips))
        step = sum(jnp.where(group == g, k, 0) for g, k in enumerate(steps))
        near = row < rows
        from_shard = jnp.where(near, d, lax.rem(d + shards - step, shards))
        from_row = jnp.where(near, row, (m ^ flip) * share + row % share)
        return pieces, from_shard, from_row, sent
    exchanged = lax.all_to_all(gradients, "dp", split_axis=1, concat_axis=0, tiled=True)
    row = jnp.arange(rows * shards, dtype=jnp.int32)
    return [exchanged], row // rows, row % rows, []


def exchange_inputs(rotated_in, shards, parts):
    d, m = lax.axis_index("dp"), lax.axis_index("mp")
    if shards == 4 and parts == 4:
        at = lambda e, p: e * parts + p
        gathered = [rotated_in]
        for k in range(1, shards):
            pairs = [(at((p + k) % shards, p), at(p, p)) for p in range(parts)]
            gathered.append(lax.ppermute(rotated_in, ("dp", "mp"), pairs))
        held = jnp.concatenate(gathered, axis=0)
        crossed = lax.ppermute(held, ("dp", "mp"), [(at(p, p), at(p, p ^ 2)) for p in range(parts)])
        held = jnp.where(m == d, held, crossed)
        swapped = lax.ppermute(
            held,
            ("dp", "mp"),
            [(at(p, p), at(p, p ^ 1)) for p in range(parts)]
            + [(at(p, p ^ 2), at(p, p ^ 3)) for p in range(parts)],
        )
        held = jnp.where((m == d) | (m == (d ^ 2)), held, swapped)
        return held, lax.rem(d + jnp.arange(shards, dtype=jnp.int32), shards)
    full = lax.all_gather(rotated_in, "mp", axis=1, tiled=True)
    held = lax.all_to_all(full, "dp", split_axis=1, concat_axis=0, tiled=True)
    return held, jnp.arange(shards, dtype=jnp.int32)


def after(x, *others):
    others = [o for o in others if o is not None]
    return lax.optimization_barrier((x, *others))[0] if others else x


def chunk_sums(rows, basis, chunks, shards):
    if shards != 4:
        return [lax.psum(rotate(rows, basis, *chunk), "dp") for chunk in chunks]
    d = lax.axis_index("dp")
    middle = (d == 1) | (d == 2)
    count = len(chunks)
    parts, inward, pairs, across, sums, outward, done = ({} for _ in range(7))

    def begin(c):
        if c < count:
            part = rotate(after(rows, parts.get(c - 1)), basis, *chunks[c])
            parts[c] = after(part, sums.get(c - AHEAD))
            inward[c] = lax.ppermute(parts[c], "dp", [(0, 1), (3, 2)])

    for c in range(AHEAD):
        begin(c)
    for s in range(count + 2):
        if s < count:
            pairs[s] = add_rounded(parts[s], after(inward[s], sums.get(s - 2)))
            across[s] = lax.ppermute(pairs[s], "dp", [(1, 2), (2, 1)])
        if 1 <= s <= count:
            sums[s - 1] = add_rounded(pairs[s - 1], after(across[s - 1], pairs.get(s)))
            outward[s - 1] = lax.ppermute(sums[s - 1], "dp", [(1, 0), (2, 3)])
            begin(s - 1 + AHEAD)
        if s >= 2:
            got = after(outward[s - 2], sums.get(s - 1))
            done[s - 2] = jnp.where(middle, sums[s - 2], got)
    return [done[c] for c in range(count)]


def rotate_and_square(
    shards, parts, bucket, places, tokens, seq_starts, seq_ends, output_basis, rotated_in, *pieces
):
    seqs = seq_starts.shape[0]
    rows = places.shape[0]
    shard_rows = rows // shards
    held, order = exchange_inputs(rotated_in, shards, parts)
    compacted = compact(pieces, places, bucket)

    window_starts = jnp.minimum(seq_starts // ALIGN * ALIGN, bucket - WINDOW)
    place = window_starts[:, None] + jnp.arange(WINDOW, dtype=jnp.int32)[None, :]
    inside = (place >= seq_starts[:, None]) & (place < seq_ends[:, None])
    token = jnp.where(inside, place + tokens[:, None], -1).reshape(-1)
    held_token = (
        order[:, None] * shard_rows + jnp.arange(shard_rows, dtype=jnp.int32)[None, :]
    ).reshape(-1)
    selector = (held_token[:, None] == token[None, :]).astype(jnp.bfloat16)
    at_windows = lax.dot_general(
        held, selector, (((0,), (0,)), ((), ())), preferred_element_type=jnp.float32
    ).astype(jnp.bfloat16)

    width = output_basis.shape[1]
    chunks = column_chunks(width)
    result = None
    for (first, _), gt_chunk in zip(chunks, chunk_sums(compacted, output_basis, chunks, shards)):
        result = squares(window_starts, at_windows, gt_chunk, 1.0 / rows, first, width, result)
    return result


def per_device(activations, gradients, input_basis, output_basis, lengths):
    groups, shards, parts = (lax.axis_size(name) for name in ("groups", "dp", "mp"))
    shard_rows = activations.shape[0]
    rows = shard_rows * shards
    seqs = lengths.shape[0]
    per_shard = seqs // shards

    pieces, from_shard, from_row, sent = exchange_gradients(gradients, shards, parts)
    rotated_in = jnp.dot(
        after(activations, *sent), input_basis, preferred_element_type=jnp.float32
    ).astype(jnp.bfloat16)

    seq_ends = jnp.cumsum(lengths, dtype=jnp.int32)
    seq_starts = seq_ends - lengths
    shard_ends = seq_ends[per_shard - 1 :: per_shard]
    shard_starts = seq_starts[::per_shard]
    tokens = (
        jnp.arange(shards, dtype=jnp.int32)[:, None] * shard_rows
        - shard_starts[:, None]
        + jnp.zeros((1, per_shard), jnp.int32)
    ).reshape(-1)
    at_shard = from_shard[:, None] == jnp.arange(shards, dtype=jnp.int32)[None, :]
    places = from_row + jnp.sum(jnp.where(at_shard, shard_starts[None, :], 0), axis=1)
    limits = jnp.sum(jnp.where(at_shard, shard_ends[None, :], 0), axis=1)
    places = jnp.where(places < limits, places, -1)

    operands = (places, tokens, seq_starts, seq_ends, output_basis, rotated_in, *pieces)
    if shards != 4 or parts != 4:
        return rotate_and_square(shards, parts, rows, *operands)
    total = seq_ends[-1:]
    if groups == 2:
        total = jnp.maximum(total, lax.ppermute(total, "groups", [(0, 1), (1, 0)]))
    elif groups > 2:
        total = lax.pmax(total, "groups")
    buckets = [rows // 16 * k for k in (6, 8, 9, 10, 11, 12, 14, 16)]
    index = sum((total[0] > size).astype(jnp.int32) for size in buckets[:-1])
    branches = [functools.partial(rotate_and_square, shards, parts, size) for size in buckets]
    return lax.switch(index, branches, *operands)


def solution(mesh):
    placed = (
        P(("groups", "dp"), None),
        P(("groups", "dp"), None),
        P(None, "mp"),
        P("dp", "mp"),
        P("groups"),
    )
    return jax.shard_map(
        per_device, mesh=mesh, in_specs=placed, out_specs=P(("groups", "dp"), "mp"), check_vma=False
    )
```

```python
import functools

import jax
import jax.numpy as jnp
from jax import lax
from jax.experimental import pallas as pl
from jax.experimental.pallas import tpu as pltpu
from jax.sharding import PartitionSpec as P

TILE = 256
WINDOW = 128
ALIGN = 16
AHEAD = 3
EDGES = (0, 3, 7, 10, 13)
MIB = 1024 * 1024


def column_chunks(width):
    tiles = -(-width // TILE)
    edges = [tiles * c // EDGES[-1] for c in EDGES]
    return [
        (lo * TILE, min(hi * TILE, width) - lo * TILE)
        for lo, hi in zip(edges[:-1], edges[1:])
        if lo < hi
    ]


def compact_kernel(pieces, place_ref, *refs):
    sources, out, buf, sems = refs[: len(pieces)], refs[-3], refs[-2], refs[-1]
    copies = []
    row = 0
    for j, size in enumerate(pieces):
        copies.append(pltpu.make_async_copy(sources[j], buf.at[pl.ds(row, size)], sems.at[j]))
        copies[-1].start()
        row += size
    place = lax.broadcasted_iota(jnp.int32, (out.shape[0], row), 0)
    selector = jnp.where(place == place_ref[...], 1.0, 0.0).astype(jnp.bfloat16)
    for copy in copies:
        copy.wait()
    width = out.shape[1]
    step = 640 if width % 640 == 0 else width
    for lo in range(0, width, step):
        out[:, lo : lo + step] = jnp.dot(
            selector, buf[:, lo : lo + step], preferred_element_type=jnp.float32
        ).astype(out.dtype)


def compact(pieces, places, rows):
    sizes = tuple(p.shape[0] for p in pieces)
    width = pieces[0].shape[1]
    return pl.pallas_call(
        functools.partial(compact_kernel, sizes),
        in_specs=[pl.BlockSpec(memory_space=pltpu.VMEM)]
        + [pl.BlockSpec(memory_space=pl.ANY)] * len(pieces),
        out_specs=pl.BlockSpec(memory_space=pltpu.VMEM),
        scratch_shapes=[
            pltpu.VMEM((sum(sizes), width), jnp.bfloat16),
            pltpu.SemaphoreType.DMA((len(pieces),)),
        ],
        out_shape=jax.ShapeDtypeStruct((rows, width), jnp.bfloat16),
        compiler_params=pltpu.CompilerParams(
            vmem_limit_bytes=2 * width * (sum(sizes) + rows) + 8 * rows * sum(sizes) + 6 * MIB
        ),
        name="compact_rows",
    )(places[None, :], *pieces)


def rotate_kernel(rows_ref, basis_ref, out_ref):
    out_ref[...] = jnp.dot(
        rows_ref[...], basis_ref[...], preferred_element_type=jnp.float32
    ).astype(out_ref.dtype)


def rotate(rows, basis, first, size):
    depth = basis.shape[0]
    begin = first // TILE
    return pl.pallas_call(
        rotate_kernel,
        grid=(-(-size // TILE),),
        in_specs=[
            pl.BlockSpec(rows.shape, lambda j: (0, 0)),
            pl.BlockSpec((depth, TILE), lambda j: (0, begin + j)),
        ],
        out_specs=pl.BlockSpec((rows.shape[0], TILE), lambda j: (0, j)),
        out_shape=jax.ShapeDtypeStruct((rows.shape[0], size), jnp.bfloat16),
        compiler_params=pltpu.CompilerParams(
            vmem_limit_bytes=4 * (rows.size + depth * TILE) + 4 * rows.shape[0] * TILE + 6 * MIB
        ),
        cost_estimate=pl.CostEstimate(flops=1, bytes_accessed=1, transcendentals=0),
        name="rotate_chunk",
    )(rows, basis)


def squares_kernel(seqs, scale, window_starts, at_ref, gt_ref, *refs):
    out_ref = refs[-1]
    for n in range(seqs):
        start = pl.multiple_of(window_starts[n], ALIGN)
        summed = jnp.dot(
            at_ref[:, n * WINDOW : (n + 1) * WINDOW],
            gt_ref[pl.ds(start, WINDOW), :],
            preferred_element_type=jnp.float32,
        )
        squared = summed * summed
        if n == 0:
            out_ref[...] = squared
        elif n < seqs - 1:
            out_ref[...] += squared
        else:
            out_ref[...] = (out_ref[...] + squared) * scale


def squares(window_starts, at_windows, gt_chunk, scale, first, total_width, previous):
    seqs = window_starts.shape[0]
    directions = at_windows.shape[0]
    rows, size = gt_chunk.shape
    begin = first // TILE
    in_specs = [
        pl.BlockSpec(at_windows.shape, lambda j, ws: (0, 0)),
        pl.BlockSpec((rows, TILE), lambda j, ws: (0, j)),
    ]
    operands = [window_starts, at_windows, gt_chunk]
    aliases = {}
    if previous is not None:
        in_specs.append(pl.BlockSpec(memory_space=pl.ANY))
        operands.append(previous)
        aliases = {3: 0}
    return pl.pallas_call(
        functools.partial(squares_kernel, seqs, scale),
        grid_spec=pltpu.PrefetchScalarGridSpec(
            num_scalar_prefetch=1,
            grid=(-(-size // TILE),),
            in_specs=in_specs,
            out_specs=pl.BlockSpec((directions, TILE), lambda j, ws: (0, begin + j)),
        ),
        out_shape=jax.ShapeDtypeStruct((directions, total_width), jnp.float32),
        input_output_aliases=aliases,
        compiler_params=pltpu.CompilerParams(
            vmem_limit_bytes=4 * (at_windows.size + rows * TILE) + 16 * directions * TILE + 6 * MIB
        ),
        cost_estimate=pl.CostEstimate(flops=1, bytes_accessed=1, transcendentals=0),
        name="sum_squares",
    )(*operands)


def exchange_gradients(gradients, shards, parts):
    d, m = lax.axis_index("dp"), lax.axis_index("mp")
    rows, hidden = gradients.shape
    width = hidden // shards
    if shards == 4 and parts == 4:
        share = rows // parts
        mine = lax.dynamic_slice_in_dim(gradients, m * share, share, 0)
        own = lax.dynamic_slice_in_dim(gradients, d * width, width, 1)
        pieces, flips, steps = [own], [], []
        far, sent = [], []
        for k in (2, 1, 3):
            block = lax.dynamic_slice_in_dim(mine, lax.rem(d + k, shards) * width, width, 1)
            sent.append(block)
            far.append(lax.ppermute(block, "dp", [(e, (e + k) % shards) for e in range(shards)]))
        for k, received in zip((2, 1, 3), far):
            crossed = lax.ppermute(received, "mp", [(p, p ^ 2) for p in range(parts)])
            pieces += [received, crossed]
            for piece in (received, crossed):
                pieces.append(lax.ppermute(piece, "mp", [(p, p ^ 1) for p in range(parts)]))
            flips += [0, 2, 1, 3]
            steps += [k] * parts
        row = jnp.arange(rows * shards, dtype=jnp.int32)
        group = jnp.maximum(row - rows, 0) // share
        flip = sum(jnp.where(group == g, f, 0) for g, f in enumerate(flips))
        step = sum(jnp.where(group == g, k, 0) for g, k in enumerate(steps))
        near = row < rows
        from_shard = jnp.where(near, d, lax.rem(d + shards - step, shards))
        from_row = jnp.where(near, row, (m ^ flip) * share + row % share)
        return pieces, from_shard, from_row, sent, pieces[10:11]
    exchanged = lax.all_to_all(gradients, "dp", split_axis=1, concat_axis=0, tiled=True)
    row = jnp.arange(rows * shards, dtype=jnp.int32)
    return [exchanged], row // rows, row % rows, [], []


def stack_kernel(*refs):
    out, row = refs[-1], 0
    for ref in refs[:-1]:
        out[row : row + ref.shape[0], :] = ref[...]
        row += ref.shape[0]


def stack(pieces):
    shape = (sum(p.shape[0] for p in pieces), pieces[0].shape[1])
    return pl.pallas_call(
        stack_kernel,
        in_specs=[pl.BlockSpec(memory_space=pltpu.VMEM)] * len(pieces),
        out_specs=pl.BlockSpec(memory_space=pltpu.VMEM),
        out_shape=jax.ShapeDtypeStruct(shape, pieces[0].dtype),
        compiler_params=pltpu.CompilerParams(vmem_limit_bytes=8 * MIB),
        name="stack_rows",
    )(*pieces)


def at(e, p, parts):
    return e * parts + p


def collect_inputs(rotated_in, shards, parts):
    if shards != 4 or parts != 4:
        full = lax.all_gather(rotated_in, "mp", axis=1, tiled=True)
        return lax.all_to_all(full, "dp", split_axis=1, concat_axis=0, tiled=True)
    gathered = [rotated_in]
    for k in range(1, shards):
        pairs = [(at((p + k) % shards, p, parts), at(p, p, parts)) for p in range(parts)]
        gathered.append(lax.ppermute(rotated_in, ("dp", "mp"), pairs))
    return stack(gathered)


def spread_inputs(held, shards, parts):
    if shards != 4 or parts != 4:
        return held, jnp.arange(shards, dtype=jnp.int32)
    d, m = lax.axis_index("dp"), lax.axis_index("mp")
    axes = ("dp", "mp")
    pairs = [(at(p, p, parts), at(p, p ^ 2, parts)) for p in range(parts)]
    held = jnp.where(m == d, held, lax.ppermute(held, axes, pairs))
    pairs = [(at(p, p ^ q, parts), at(p, p ^ q ^ 1, parts)) for p in range(parts) for q in (0, 2)]
    swapped = lax.ppermute(held, axes, pairs)
    held = jnp.where((m == d) | (m == (d ^ 2)), held, swapped)
    return held, lax.rem(d + jnp.arange(shards, dtype=jnp.int32), shards)


def add_rounded(a, b):
    return (a.astype(jnp.float32) + b.astype(jnp.float32)).astype(jnp.bfloat16)


def after(x, *others):
    others = [o for o in others if o is not None]
    return lax.optimization_barrier((x, *others))[0] if others else x


def chunk_sums(rows, basis, chunks, shards):
    if shards != 4:
        return [lax.psum(rotate(rows, basis, *chunk), "dp") for chunk in chunks]
    d = lax.axis_index("dp")
    middle = (d == 1) | (d == 2)
    count = len(chunks)
    parts, inward, pairs, across, sums, outward, done = ({} for _ in range(7))

    def begin(c):
        if c < count:
            part = rotate(after(rows, parts.get(c - 1)), basis, *chunks[c])
            parts[c] = after(part, sums.get(c - AHEAD))
            inward[c] = lax.ppermute(parts[c], "dp", [(0, 1), (3, 2)])

    for c in range(AHEAD):
        begin(c)
    for s in range(count + 2):
        if s < count:
            pairs[s] = add_rounded(parts[s], after(inward[s], sums.get(s - 2), done.get(s - 3)))
            across[s] = lax.ppermute(pairs[s], "dp", [(1, 2), (2, 1)])
        if 1 <= s <= count:
            sums[s - 1] = add_rounded(pairs[s - 1], after(across[s - 1], pairs.get(s)))
            outward[s - 1] = lax.ppermute(sums[s - 1], "dp", [(1, 0), (2, 3)])
            begin(s - 1 + AHEAD)
        if s >= 2:
            got = after(outward[s - 2], sums.get(s - 1))
            done[s - 2] = jnp.where(middle, sums[s - 2], got)
    return [after(done[c], sums[min(c + 3, count - 1)]) for c in range(count)]


def rotate_and_square(
    shards, parts, bucket, places, tokens, seq_starts, seq_ends, output_basis, held, *pieces
):
    seqs = seq_starts.shape[0]
    rows = places.shape[0]
    shard_rows = rows // shards
    held, order = spread_inputs(collect_inputs(held, shards, parts), shards, parts)
    compacted = compact(pieces, places, bucket)

    window_starts = jnp.minimum(seq_starts // ALIGN * ALIGN, bucket - WINDOW)
    place = window_starts[:, None] + jnp.arange(WINDOW, dtype=jnp.int32)[None, :]
    inside = (place >= seq_starts[:, None]) & (place < seq_ends[:, None])
    token = jnp.where(inside, place + tokens[:, None], -1).reshape(-1)
    held_token = (
        order[:, None] * shard_rows + jnp.arange(shard_rows, dtype=jnp.int32)[None, :]
    ).reshape(-1)
    selector = (held_token[:, None] == token[None, :]).astype(jnp.bfloat16)
    at_windows = lax.dot_general(
        held, selector, (((0,), (0,)), ((), ())), preferred_element_type=jnp.float32
    ).astype(jnp.bfloat16)

    width = output_basis.shape[1]
    chunks = column_chunks(width)
    result = None
    for (first, _), gt_chunk in zip(chunks, chunk_sums(compacted, output_basis, chunks, shards)):
        result = squares(window_starts, at_windows, gt_chunk, 1.0 / rows, first, width, result)
    return result


def per_device(activations, gradients, input_basis, output_basis, lengths):
    groups, shards, parts = (lax.axis_size(name) for name in ("groups", "dp", "mp"))
    shard_rows = activations.shape[0]
    rows = shard_rows * shards
    seqs = lengths.shape[0]
    per_shard = seqs // shards

    pieces, from_shard, from_row, sent, crossed = exchange_gradients(gradients, shards, parts)
    rotated_in = jnp.dot(
        after(activations, *sent), input_basis, preferred_element_type=jnp.float32
    ).astype(jnp.bfloat16)

    seq_ends = jnp.cumsum(lengths, dtype=jnp.int32)
    seq_starts = seq_ends - lengths
    shard_ends = seq_ends[per_shard - 1 :: per_shard]
    shard_starts = seq_starts[::per_shard]
    tokens = (
        jnp.arange(shards, dtype=jnp.int32)[:, None] * shard_rows
        - shard_starts[:, None]
        + jnp.zeros((1, per_shard), jnp.int32)
    ).reshape(-1)
    at_shard = from_shard[:, None] == jnp.arange(shards, dtype=jnp.int32)[None, :]
    places = from_row + jnp.sum(jnp.where(at_shard, shard_starts[None, :], 0), axis=1)
    limits = jnp.sum(jnp.where(at_shard, shard_ends[None, :], 0), axis=1)
    places = jnp.where(places < limits, places, -1)

    held = rotated_in
    operands = lax.optimization_barrier((places, tokens, seq_starts, seq_ends, output_basis, held, *pieces))
    if shards != 4 or parts != 4:
        return rotate_and_square(shards, parts, rows, *operands)
    total = seq_ends[-1:]
    if groups == 2:
        total = jnp.maximum(total, lax.ppermute(total, "groups", [(0, 1), (1, 0)]))
    elif groups > 2:
        total = lax.pmax(total, "groups")
    buckets = [rows // 16 * k for k in (11, 16)]
    index = sum((total[0] > size).astype(jnp.int32) for size in buckets[:-1])
    branches = [functools.partial(rotate_and_square, shards, parts, size) for size in buckets]
    return lax.switch(index, branches, *operands)


def solution(mesh):
    placed = (
        P(("groups", "dp"), None),
        P(("groups", "dp"), None),
        P(None, "mp"),
        P("dp", "mp"),
        P("groups"),
    )
    return jax.shard_map(
        per_device, mesh=mesh, in_specs=placed, out_specs=P(("groups", "dp"), "mp"), check_vma=False
    )
```

```python
import functools

import jax
import jax.numpy as jnp
from jax import lax
from jax.experimental import pallas as pl
from jax.experimental.pallas import tpu as pltpu
from jax.sharding import PartitionSpec as P

TILE = 256
WINDOW = 128
ALIGN = 16
AHEAD = 4
STARTED = 1
EDGES = (0, 3, 7, 10, 13)
FEW_EDGES = (0, 6, 13)
MIB = 1024 * 1024


def column_chunks(width, marks):
    tiles = -(-width // TILE)
    edges = [tiles * c // marks[-1] for c in marks]
    return [
        (lo * TILE, min(hi * TILE, width) - lo * TILE)
        for lo, hi in zip(edges[:-1], edges[1:])
        if lo < hi
    ]


def compact_kernel(pieces, place_ref, *refs):
    sources, out, buf, sems = refs[: len(pieces)], refs[-3], refs[-2], refs[-1]
    copies = []
    row = 0
    for j, size in enumerate(pieces):
        copies.append(pltpu.make_async_copy(sources[j], buf.at[pl.ds(row, size)], sems.at[j]))
        copies[-1].start()
        row += size
    place = lax.broadcasted_iota(jnp.int32, (out.shape[0], row), 0)
    selector = jnp.where(place == place_ref[...], 1.0, 0.0).astype(jnp.bfloat16)
    for copy in copies:
        copy.wait()
    width = out.shape[1]
    step = 640 if width % 640 == 0 else width
    for lo in range(0, width, step):
        out[:, lo : lo + step] = jnp.dot(
            selector, buf[:, lo : lo + step], preferred_element_type=jnp.float32
        ).astype(out.dtype)


def compact(pieces, places, rows):
    sizes = tuple(p.shape[0] for p in pieces)
    width = pieces[0].shape[1]
    return pl.pallas_call(
        functools.partial(compact_kernel, sizes),
        in_specs=[pl.BlockSpec(memory_space=pltpu.VMEM)]
        + [pl.BlockSpec(memory_space=pl.ANY)] * len(pieces),
        out_specs=pl.BlockSpec(memory_space=pltpu.VMEM),
        scratch_shapes=[
            pltpu.VMEM((sum(sizes), width), jnp.bfloat16),
            pltpu.SemaphoreType.DMA((len(pieces),)),
        ],
        out_shape=jax.ShapeDtypeStruct((rows, width), jnp.bfloat16),
        compiler_params=pltpu.CompilerParams(
            vmem_limit_bytes=2 * width * (sum(sizes) + rows) + 8 * rows * sum(sizes) + 6 * MIB
        ),
        name="compact_rows",
    )(places[None, :], *pieces)


def rotate_kernel(rows_ref, basis_ref, out_ref):
    out_ref[...] = jnp.dot(
        rows_ref[...], basis_ref[...], preferred_element_type=jnp.float32
    ).astype(out_ref.dtype)


def rotate(rows, basis, first, size):
    depth = basis.shape[0]
    begin = first // TILE
    return pl.pallas_call(
        rotate_kernel,
        grid=(-(-size // TILE),),
        in_specs=[
            pl.BlockSpec(rows.shape, lambda j: (0, 0)),
            pl.BlockSpec((depth, TILE), lambda j: (0, begin + j)),
        ],
        out_specs=pl.BlockSpec((rows.shape[0], TILE), lambda j: (0, j)),
        out_shape=jax.ShapeDtypeStruct((rows.shape[0], size), jnp.bfloat16),
        compiler_params=pltpu.CompilerParams(
            vmem_limit_bytes=4 * (rows.size + depth * TILE) + 4 * rows.shape[0] * TILE + 6 * MIB
        ),
        cost_estimate=pl.CostEstimate(flops=1, bytes_accessed=1, transcendentals=0),
        name="rotate_chunk",
    )(rows, basis)


def squares_kernel(seqs, scale, window_starts, at_ref, gt_ref, *refs):
    out_ref = refs[-1]
    for n in range(seqs):
        start = pl.multiple_of(window_starts[n], ALIGN)
        summed = jnp.dot(
            at_ref[:, n * WINDOW : (n + 1) * WINDOW],
            gt_ref[pl.ds(start, WINDOW), :],
            preferred_element_type=jnp.float32,
        )
        squared = summed * summed
        if n == 0:
            out_ref[...] = squared
        elif n < seqs - 1:
            out_ref[...] += squared
        else:
            out_ref[...] = (out_ref[...] + squared) * scale


def squares(window_starts, at_windows, gt_chunk, scale, first, total_width, previous):
    seqs = window_starts.shape[0]
    directions = at_windows.shape[0]
    rows, size = gt_chunk.shape
    begin = first // TILE
    in_specs = [
        pl.BlockSpec(at_windows.shape, lambda j, ws: (0, 0)),
        pl.BlockSpec((rows, TILE), lambda j, ws: (0, j)),
    ]
    operands = [window_starts, at_windows, gt_chunk]
    aliases = {}
    if previous is not None:
        in_specs.append(pl.BlockSpec(memory_space=pl.ANY))
        operands.append(previous)
        aliases = {3: 0}
    return pl.pallas_call(
        functools.partial(squares_kernel, seqs, scale),
        grid_spec=pltpu.PrefetchScalarGridSpec(
            num_scalar_prefetch=1,
            grid=(-(-size // TILE),),
            in_specs=in_specs,
            out_specs=pl.BlockSpec((directions, TILE), lambda j, ws: (0, begin + j)),
        ),
        out_shape=jax.ShapeDtypeStruct((directions, total_width), jnp.float32),
        input_output_aliases=aliases,
        compiler_params=pltpu.CompilerParams(
            vmem_limit_bytes=4 * (at_windows.size + rows * TILE) + 16 * directions * TILE + 6 * MIB
        ),
        cost_estimate=pl.CostEstimate(flops=1, bytes_accessed=1, transcendentals=0),
        name="sum_squares",
    )(*operands)


def exchange_gradients(gradients, shards, parts):
    d, m = lax.axis_index("dp"), lax.axis_index("mp")
    rows, hidden = gradients.shape
    width = hidden // shards
    if shards == 4 and parts == 4:
        share = rows // parts
        mine = lax.dynamic_slice_in_dim(gradients, m * share, share, 0)
        own = lax.dynamic_slice_in_dim(gradients, d * width, width, 1)
        pieces, flips, steps = [own], [], []
        far, sent = [], []
        for k in (2, 1, 3):
            block = lax.dynamic_slice_in_dim(mine, lax.rem(d + k, shards) * width, width, 1)
            sent.append(block)
            far.append(lax.ppermute(block, "dp", [(e, (e + k) % shards) for e in range(shards)]))
        for k, received in zip((2, 1, 3), far):
            crossed = lax.ppermute(received, "mp", [(p, p ^ 2) for p in range(parts)])
            pieces += [received, crossed]
            for piece in (received, crossed):
                pieces.append(lax.ppermute(piece, "mp", [(p, p ^ 1) for p in range(parts)]))
            flips += [0, 2, 1, 3]
            steps += [k] * parts
        row = jnp.arange(rows * shards, dtype=jnp.int32)
        group = jnp.maximum(row - rows, 0) // share
        flip = sum(jnp.where(group == g, f, 0) for g, f in enumerate(flips))
        step = sum(jnp.where(group == g, k, 0) for g, k in enumerate(steps))
        near = row < rows
        from_shard = jnp.where(near, d, lax.rem(d + shards - step, shards))
        from_row = jnp.where(near, row, (m ^ flip) * share + row % share)
        return pieces, from_shard, from_row, sent, pieces[10:11]
    exchanged = lax.all_to_all(gradients, "dp", split_axis=1, concat_axis=0, tiled=True)
    row = jnp.arange(rows * shards, dtype=jnp.int32)
    return [exchanged], row // rows, row % rows, [], []


def stack_kernel(*refs):
    out, row = refs[-1], 0
    for ref in refs[:-1]:
        out[row : row + ref.shape[0], :] = ref[...]
        row += ref.shape[0]


def stack(pieces):
    shape = (sum(p.shape[0] for p in pieces), pieces[0].shape[1])
    return pl.pallas_call(
        stack_kernel,
        in_specs=[pl.BlockSpec(memory_space=pltpu.VMEM)] * len(pieces),
        out_specs=pl.BlockSpec(memory_space=pltpu.VMEM),
        out_shape=jax.ShapeDtypeStruct(shape, pieces[0].dtype),
        compiler_params=pltpu.CompilerParams(vmem_limit_bytes=8 * MIB),
        name="stack_rows",
    )(*pieces)


def at(e, p, parts):
    return e * parts + p


def collect_inputs(rotated_in, shards, parts):
    if shards != 4 or parts != 4:
        full = lax.all_gather(rotated_in, "mp", axis=1, tiled=True)
        return lax.all_to_all(full, "dp", split_axis=1, concat_axis=0, tiled=True)
    gathered = [rotated_in]
    for k in range(1, shards):
        pairs = [(at((p + k) % shards, p, parts), at(p, p, parts)) for p in range(parts)]
        gathered.append(lax.ppermute(rotated_in, ("dp", "mp"), pairs))
    return stack(gathered)


def spread_inputs(held, shards, parts):
    if shards != 4 or parts != 4:
        return held, jnp.arange(shards, dtype=jnp.int32)
    d, m = lax.axis_index("dp"), lax.axis_index("mp")
    axes = ("dp", "mp")
    pairs = [(at(p, p, parts), at(p, p ^ 2, parts)) for p in range(parts)]
    held = jnp.where(m == d, held, lax.ppermute(held, axes, pairs))
    pairs = [(at(p, p ^ q, parts), at(p, p ^ q ^ 1, parts)) for p in range(parts) for q in (0, 2)]
    swapped = lax.ppermute(held, axes, pairs)
    held = jnp.where((m == d) | (m == (d ^ 2)), held, swapped)
    return held, lax.rem(d + jnp.arange(shards, dtype=jnp.int32), shards)


def add_rounded(a, b):
    return (a.astype(jnp.float32) + b.astype(jnp.float32)).astype(jnp.bfloat16)


def after(x, *others):
    others = [o for o in others if o is not None]
    return lax.optimization_barrier((x, *others))[0] if others else x


def chunk_sums(rows, basis, chunks, shards, started):
    if shards != 4:
        parts = started + [rotate(rows, basis, *chunk) for chunk in chunks[len(started) :]]
        return [lax.psum(part, "dp") for part in parts]
    d = lax.axis_index("dp")
    middle = (d == 1) | (d == 2)
    count = len(chunks)
    parts, inward, pairs, across, sums, outward, done = ({} for _ in range(7))

    def begin(c):
        if c < count:
            if c < len(started):
                part = started[c]
            else:
                part = rotate(after(rows, parts.get(c - 1)), basis, *chunks[c])
            parts[c] = after(part, sums.get(c - AHEAD))
            inward[c] = lax.ppermute(parts[c], "dp", [(0, 1), (3, 2)])

    for c in range(AHEAD):
        begin(c)
    for s in range(count + 2):
        if s < count:
            pairs[s] = add_rounded(parts[s], after(inward[s], sums.get(s - 2), done.get(s - 3)))
            across[s] = lax.ppermute(pairs[s], "dp", [(1, 2), (2, 1)])
        if 1 <= s <= count:
            sums[s - 1] = add_rounded(pairs[s - 1], after(across[s - 1], pairs.get(s)))
            outward[s - 1] = lax.ppermute(sums[s - 1], "dp", [(1, 0), (2, 3)])
            begin(s - 1 + AHEAD)
        if s >= 2:
            got = after(outward[s - 2], sums.get(s - 1))
            done[s - 2] = jnp.where(middle, sums[s - 2], got)
    return [after(done[c], sums[min(c + 3, count - 1)]) for c in range(count)]


def rotate_and_square(
    shards, parts, bucket, places, tokens, seq_starts, seq_ends, output_basis, held, *pieces
):
    seqs = seq_starts.shape[0]
    rows = places.shape[0]
    shard_rows = rows // shards
    compacted = compact(pieces, places, bucket)
    width = output_basis.shape[1]
    chunks = column_chunks(width, EDGES if bucket < rows else FEW_EDGES)
    started = []
    for chunk in chunks[:STARTED]:
        started.append(rotate(after(compacted, *started[-1:]), output_basis, *chunk))
    held = after(held, *started[-1:])
    held, order = spread_inputs(collect_inputs(held, shards, parts), shards, parts)

    window_starts = jnp.minimum(seq_starts // ALIGN * ALIGN, bucket - WINDOW)
    place = window_starts[:, None] + jnp.arange(WINDOW, dtype=jnp.int32)[None, :]
    inside = (place >= seq_starts[:, None]) & (place < seq_ends[:, None])
    token = jnp.where(inside, place + tokens[:, None], -1).reshape(-1)
    held_token = (
        order[:, None] * shard_rows + jnp.arange(shard_rows, dtype=jnp.int32)[None, :]
    ).reshape(-1)
    selector = (held_token[:, None] == token[None, :]).astype(jnp.bfloat16)
    at_windows = lax.dot_general(
        held, selector, (((0,), (0,)), ((), ())), preferred_element_type=jnp.float32
    ).astype(jnp.bfloat16)

    sums = chunk_sums(compacted, output_basis, chunks, shards, started)
    result = None
    for (first, _), gt_chunk in zip(chunks, sums):
        result = squares(window_starts, at_windows, gt_chunk, 1.0 / rows, first, width, result)
    return result


def per_device(activations, gradients, input_basis, output_basis, lengths):
    groups, shards, parts = (lax.axis_size(name) for name in ("groups", "dp", "mp"))
    shard_rows = activations.shape[0]
    rows = shard_rows * shards
    seqs = lengths.shape[0]
    per_shard = seqs // shards

    pieces, from_shard, from_row, sent, crossed = exchange_gradients(gradients, shards, parts)
    rotated_in = jnp.dot(
        after(activations, *sent), input_basis, preferred_element_type=jnp.float32
    ).astype(jnp.bfloat16)

    seq_ends = jnp.cumsum(lengths, dtype=jnp.int32)
    seq_starts = seq_ends - lengths
    shard_ends = seq_ends[per_shard - 1 :: per_shard]
    shard_starts = seq_starts[::per_shard]
    tokens = (
        jnp.arange(shards, dtype=jnp.int32)[:, None] * shard_rows
        - shard_starts[:, None]
        + jnp.zeros((1, per_shard), jnp.int32)
    ).reshape(-1)
    at_shard = from_shard[:, None] == jnp.arange(shards, dtype=jnp.int32)[None, :]
    places = from_row + jnp.sum(jnp.where(at_shard, shard_starts[None, :], 0), axis=1)
    limits = jnp.sum(jnp.where(at_shard, shard_ends[None, :], 0), axis=1)
    places = jnp.where(places < limits, places, -1)

    held = rotated_in
    operands = lax.optimization_barrier((places, tokens, seq_starts, seq_ends, output_basis, held, *pieces))
    if shards != 4 or parts != 4:
        return rotate_and_square(shards, parts, rows, *operands)
    total = after(seq_ends[-1:], rotated_in)
    if groups == 2:
        total = jnp.maximum(total, lax.ppermute(total, "groups", [(0, 1), (1, 0)]))
    elif groups > 2:
        total = lax.pmax(total, "groups")
    buckets = [rows // 16 * k for k in (11, 16)]
    index = sum((total[0] > size).astype(jnp.int32) for size in buckets[:-1])
    branches = [functools.partial(rotate_and_square, shards, parts, size) for size in buckets]
    return lax.switch(index, branches, *operands)


def solution(mesh):
    placed = (
        P(("groups", "dp"), None),
        P(("groups", "dp"), None),
        P(None, "mp"),
        P("dp", "mp"),
        P("groups"),
    )
    return jax.shard_map(
        per_device, mesh=mesh, in_specs=placed, out_specs=P(("groups", "dp"), "mp"), check_vma=False
    )
```

```python
import functools

import jax
import jax.numpy as jnp
from jax import lax
from jax.experimental import pallas as pl
from jax.experimental.pallas import tpu as pltpu
from jax.sharding import PartitionSpec as P

TILE = 256
WINDOW = 128
ALIGN = 16
AHEAD = 4
STARTED = 1
EDGES = (0, 3, 7, 10, 13)
FEW_EDGES = (0, 6, 13)
MIB = 1024 * 1024


def column_chunks(width, marks):
    tiles = -(-width // TILE)
    edges = [tiles * c // marks[-1] for c in marks]
    return [
        (lo * TILE, min(hi * TILE, width) - lo * TILE)
        for lo, hi in zip(edges[:-1], edges[1:])
        if lo < hi
    ]


def compact_kernel(pieces, place_ref, *refs):
    sources, out, buf, sems = refs[: len(pieces)], refs[-3], refs[-2], refs[-1]
    copies = []
    row = 0
    for j, size in enumerate(pieces):
        copies.append(pltpu.make_async_copy(sources[j], buf.at[pl.ds(row, size)], sems.at[j]))
        copies[-1].start()
        row += size
    place = lax.broadcasted_iota(jnp.int32, (out.shape[0], row), 0)
    selector = jnp.where(place == place_ref[...], 1.0, 0.0).astype(jnp.bfloat16)
    for copy in copies:
        copy.wait()
    width = out.shape[1]
    step = 640 if width % 640 == 0 else width
    for lo in range(0, width, step):
        out[:, lo : lo + step] = jnp.dot(
            selector, buf[:, lo : lo + step], preferred_element_type=jnp.float32
        ).astype(out.dtype)


def compact(pieces, places, rows):
    sizes = tuple(p.shape[0] for p in pieces)
    width = pieces[0].shape[1]
    return pl.pallas_call(
        functools.partial(compact_kernel, sizes),
        in_specs=[pl.BlockSpec(memory_space=pltpu.VMEM)]
        + [pl.BlockSpec(memory_space=pl.ANY)] * len(pieces),
        out_specs=pl.BlockSpec(memory_space=pltpu.VMEM),
        scratch_shapes=[
            pltpu.VMEM((sum(sizes), width), jnp.bfloat16),
            pltpu.SemaphoreType.DMA((len(pieces),)),
        ],
        out_shape=jax.ShapeDtypeStruct((rows, width), jnp.bfloat16),
        compiler_params=pltpu.CompilerParams(
            vmem_limit_bytes=2 * width * (sum(sizes) + rows) + 8 * rows * sum(sizes) + 6 * MIB
        ),
        name="compact_rows",
    )(places[None, :], *pieces)


def rotate_kernel(rows_ref, basis_ref, out_ref):
    out_ref[...] = jnp.dot(
        rows_ref[...], basis_ref[...], preferred_element_type=jnp.float32
    ).astype(out_ref.dtype)


def rotate(rows, basis, first, size):
    depth = basis.shape[0]
    begin = first // TILE
    return pl.pallas_call(
        rotate_kernel,
        grid=(-(-size // TILE),),
        in_specs=[
            pl.BlockSpec(rows.shape, lambda j: (0, 0)),
            pl.BlockSpec((depth, TILE), lambda j: (0, begin + j)),
        ],
        out_specs=pl.BlockSpec((rows.shape[0], TILE), lambda j: (0, j)),
        out_shape=jax.ShapeDtypeStruct((rows.shape[0], size), jnp.bfloat16),
        compiler_params=pltpu.CompilerParams(
            vmem_limit_bytes=4 * (rows.size + depth * TILE) + 4 * rows.shape[0] * TILE + 6 * MIB
        ),
        cost_estimate=pl.CostEstimate(flops=1, bytes_accessed=1, transcendentals=0),
        name="rotate_chunk",
    )(rows, basis)


def squares_kernel(seqs, scale, window_starts, at_ref, gt_ref, *refs):
    out_ref = refs[-1]
    for n in range(seqs):
        start = pl.multiple_of(window_starts[n], ALIGN)
        summed = jnp.dot(
            at_ref[:, n * WINDOW : (n + 1) * WINDOW],
            gt_ref[pl.ds(start, WINDOW), :],
            preferred_element_type=jnp.float32,
        )
        squared = summed * summed
        if n == 0:
            out_ref[...] = squared
        elif n < seqs - 1:
            out_ref[...] += squared
        else:
            out_ref[...] = (out_ref[...] + squared) * scale


def squares(window_starts, at_windows, gt_chunk, scale, first, total_width, previous):
    seqs = window_starts.shape[0]
    directions = at_windows.shape[0]
    rows, size = gt_chunk.shape
    begin = first // TILE
    in_specs = [
        pl.BlockSpec(at_windows.shape, lambda j, ws: (0, 0)),
        pl.BlockSpec((rows, TILE), lambda j, ws: (0, j)),
    ]
    operands = [window_starts, at_windows, gt_chunk]
    aliases = {}
    if previous is not None:
        in_specs.append(pl.BlockSpec(memory_space=pl.ANY))
        operands.append(previous)
        aliases = {3: 0}
    return pl.pallas_call(
        functools.partial(squares_kernel, seqs, scale),
        grid_spec=pltpu.PrefetchScalarGridSpec(
            num_scalar_prefetch=1,
            grid=(-(-size // TILE),),
            in_specs=in_specs,
            out_specs=pl.BlockSpec((directions, TILE), lambda j, ws: (0, begin + j)),
        ),
        out_shape=jax.ShapeDtypeStruct((directions, total_width), jnp.float32),
        input_output_aliases=aliases,
        compiler_params=pltpu.CompilerParams(
            vmem_limit_bytes=4 * (at_windows.size + rows * TILE) + 16 * directions * TILE + 6 * MIB
        ),
        cost_estimate=pl.CostEstimate(flops=1, bytes_accessed=1, transcendentals=0),
        name="sum_squares",
    )(*operands)


def exchange_gradients(gradients, shards, parts):
    d, m = lax.axis_index("dp"), lax.axis_index("mp")
    rows, hidden = gradients.shape
    width = hidden // shards
    if shards == 4 and parts == 4:
        share = rows // parts
        mine = lax.dynamic_slice_in_dim(gradients, m * share, share, 0)
        own = lax.dynamic_slice_in_dim(gradients, d * width, width, 1)
        pieces, flips, steps = [own], [], []
        far, sent = [], []
        for k in (2, 1, 3):
            block = lax.dynamic_slice_in_dim(mine, lax.rem(d + k, shards) * width, width, 1)
            sent.append(block)
            far.append(lax.ppermute(block, "dp", [(e, (e + k) % shards) for e in range(shards)]))
        for k, received in zip((2, 1, 3), far):
            crossed = lax.ppermute(received, "mp", [(p, p ^ 2) for p in range(parts)])
            pieces += [received, crossed]
            for piece in (received, crossed):
                pieces.append(lax.ppermute(piece, "mp", [(p, p ^ 1) for p in range(parts)]))
            flips += [0, 2, 1, 3]
            steps += [k] * parts
        row = jnp.arange(rows * shards, dtype=jnp.int32)
        group = jnp.maximum(row - rows, 0) // share
        flip = sum(jnp.where(group == g, f, 0) for g, f in enumerate(flips))
        step = sum(jnp.where(group == g, k, 0) for g, k in enumerate(steps))
        near = row < rows
        from_shard = jnp.where(near, d, lax.rem(d + shards - step, shards))
        from_row = jnp.where(near, row, (m ^ flip) * share + row % share)
        return pieces, from_shard, from_row, sent, pieces[10:11]
    exchanged = lax.all_to_all(gradients, "dp", split_axis=1, concat_axis=0, tiled=True)
    row = jnp.arange(rows * shards, dtype=jnp.int32)
    return [exchanged], row // rows, row % rows, [], []


def stack_kernel(*refs):
    out, row = refs[-1], 0
    for ref in refs[:-1]:
        out[row : row + ref.shape[0], :] = ref[...]
        row += ref.shape[0]


def stack(pieces):
    shape = (sum(p.shape[0] for p in pieces), pieces[0].shape[1])
    return pl.pallas_call(
        stack_kernel,
        in_specs=[pl.BlockSpec(memory_space=pltpu.VMEM)] * len(pieces),
        out_specs=pl.BlockSpec(memory_space=pltpu.VMEM),
        out_shape=jax.ShapeDtypeStruct(shape, pieces[0].dtype),
        compiler_params=pltpu.CompilerParams(vmem_limit_bytes=8 * MIB),
        name="stack_rows",
    )(*pieces)


def at(e, p, parts):
    return e * parts + p


def collect_inputs(rotated_in, shards, parts):
    if shards != 4 or parts != 4:
        full = lax.all_gather(rotated_in, "mp", axis=1, tiled=True)
        return lax.all_to_all(full, "dp", split_axis=1, concat_axis=0, tiled=True)
    gathered = [rotated_in]
    for k in range(1, shards):
        pairs = [(at((p + k) % shards, p, parts), at(p, p, parts)) for p in range(parts)]
        gathered.append(lax.ppermute(rotated_in, ("dp", "mp"), pairs))
    return stack(gathered)


def spread_inputs(held, shards, parts):
    if shards != 4 or parts != 4:
        return held, jnp.arange(shards, dtype=jnp.int32)
    d, m = lax.axis_index("dp"), lax.axis_index("mp")
    axes = ("dp", "mp")
    pairs = [(at(p, p, parts), at(p, p ^ 2, parts)) for p in range(parts)]
    held = jnp.where(m == d, held, lax.ppermute(held, axes, pairs))
    pairs = [(at(p, p ^ q, parts), at(p, p ^ q ^ 1, parts)) for p in range(parts) for q in (0, 2)]
    swapped = lax.ppermute(held, axes, pairs)
    held = jnp.where((m == d) | (m == (d ^ 2)), held, swapped)
    return held, lax.rem(d + jnp.arange(shards, dtype=jnp.int32), shards)


def add_rounded(a, b):
    return (a.astype(jnp.float32) + b.astype(jnp.float32)).astype(jnp.bfloat16)


def after(x, *others):
    others = [o for o in others if o is not None]
    return lax.optimization_barrier((x, *others))[0] if others else x


def chunk_sums(rows, basis, chunks, shards, started):
    if shards != 4:
        parts = started + [rotate(rows, basis, *chunk) for chunk in chunks[len(started) :]]
        return [lax.psum(part, "dp") for part in parts]
    d = lax.axis_index("dp")
    middle = (d == 1) | (d == 2)
    count = len(chunks)
    parts, inward, pairs, across, sums, outward, done = ({} for _ in range(7))

    def begin(c):
        if c < count:
            if c < len(started):
                part = started[c]
            else:
                part = rotate(after(rows, parts.get(c - 1)), basis, *chunks[c])
            parts[c] = after(part, sums.get(c - AHEAD))
            inward[c] = lax.ppermute(parts[c], "dp", [(0, 1), (3, 2)])

    for c in range(AHEAD):
        begin(c)
    for s in range(count + 2):
        if s < count:
            pairs[s] = add_rounded(parts[s], after(inward[s], sums.get(s - 2), done.get(s - 3)))
            across[s] = lax.ppermute(pairs[s], "dp", [(1, 2), (2, 1)])
        if 1 <= s <= count:
            sums[s - 1] = add_rounded(pairs[s - 1], after(across[s - 1], pairs.get(s)))
            outward[s - 1] = lax.ppermute(sums[s - 1], "dp", [(1, 0), (2, 3)])
            begin(s - 1 + AHEAD)
        if s >= 2:
            got = after(outward[s - 2], sums.get(s - 1))
            done[s - 2] = jnp.where(middle, sums[s - 2], got)
    return [after(done[c], sums[min(c + 2, count - 1)]) for c in range(count)]


def rotate_and_square(
    shards, parts, bucket, places, tokens, seq_starts, seq_ends, output_basis, held, *pieces
):
    seqs = seq_starts.shape[0]
    rows = places.shape[0]
    shard_rows = rows // shards
    compacted = compact(pieces, places, bucket)
    width = output_basis.shape[1]
    chunks = column_chunks(width, EDGES if bucket < rows else FEW_EDGES)
    started = []
    for chunk in chunks[:STARTED]:
        started.append(rotate(after(compacted, *started[-1:]), output_basis, *chunk))
    held = after(held, *started[-1:])
    held, order = spread_inputs(collect_inputs(held, shards, parts), shards, parts)

    window_starts = jnp.minimum(seq_starts // ALIGN * ALIGN, bucket - WINDOW)
    place = window_starts[:, None] + jnp.arange(WINDOW, dtype=jnp.int32)[None, :]
    inside = (place >= seq_starts[:, None]) & (place < seq_ends[:, None])
    token = jnp.where(inside, place + tokens[:, None], -1).reshape(-1)
    held_token = (
        order[:, None] * shard_rows + jnp.arange(shard_rows, dtype=jnp.int32)[None, :]
    ).reshape(-1)
    selector = (held_token[:, None] == token[None, :]).astype(jnp.bfloat16)
    at_windows = lax.dot_general(
        held, selector, (((0,), (0,)), ((), ())), preferred_element_type=jnp.float32
    ).astype(jnp.bfloat16)

    sums = chunk_sums(compacted, output_basis, chunks, shards, started)
    result = None
    for (first, _), gt_chunk in zip(chunks, sums):
        result = squares(window_starts, at_windows, gt_chunk, 1.0 / rows, first, width, result)
    return result


def per_device(activations, gradients, input_basis, output_basis, lengths):
    groups, shards, parts = (lax.axis_size(name) for name in ("groups", "dp", "mp"))
    shard_rows = activations.shape[0]
    rows = shard_rows * shards
    seqs = lengths.shape[0]
    per_shard = seqs // shards

    pieces, from_shard, from_row, sent, crossed = exchange_gradients(gradients, shards, parts)
    rotated_in = jnp.dot(
        after(activations, *sent), input_basis, preferred_element_type=jnp.float32
    ).astype(jnp.bfloat16)

    seq_ends = jnp.cumsum(lengths, dtype=jnp.int32)
    seq_starts = seq_ends - lengths
    shard_ends = seq_ends[per_shard - 1 :: per_shard]
    shard_starts = seq_starts[::per_shard]
    tokens = (
        jnp.arange(shards, dtype=jnp.int32)[:, None] * shard_rows
        - shard_starts[:, None]
        + jnp.zeros((1, per_shard), jnp.int32)
    ).reshape(-1)
    at_shard = from_shard[:, None] == jnp.arange(shards, dtype=jnp.int32)[None, :]
    places = from_row + jnp.sum(jnp.where(at_shard, shard_starts[None, :], 0), axis=1)
    limits = jnp.sum(jnp.where(at_shard, shard_ends[None, :], 0), axis=1)
    places = jnp.where(places < limits, places, -1)

    held = rotated_in
    operands = lax.optimization_barrier((places, tokens, seq_starts, seq_ends, output_basis, held, *pieces))
    if shards != 4 or parts != 4:
        return rotate_and_square(shards, parts, rows, *operands)
    total = after(seq_ends[-1:], rotated_in)
    if groups == 2:
        total = jnp.maximum(total, lax.ppermute(total, "groups", [(0, 1), (1, 0)]))
    elif groups > 2:
        total = lax.pmax(total, "groups")
    buckets = [rows // 16 * k for k in (11, 16)]
    index = sum((total[0] > size).astype(jnp.int32) for size in buckets[:-1])
    branches = [functools.partial(rotate_and_square, shards, parts, size) for size in buckets]
    return lax.switch(index, branches, *operands)


def solution(mesh):
    placed = (
        P(("groups", "dp"), None),
        P(("groups", "dp"), None),
        P(None, "mp"),
        P("dp", "mp"),
        P("groups"),
    )
    return jax.shard_map(
        per_device, mesh=mesh, in_specs=placed, out_specs=P(("groups", "dp"), "mp"), check_vma=False
    )
```
